512 devices in a mesh: mirror: 32 (over z, y_hi), request: 8 (over x, y_lo), tensor: 2 (over core).
Axes of the slice: x: 4, y: 4 (y_hi: 2, y_lo: 2; y = y_hi * 2 + y_lo), z: 16, core: 2. Of those that a mesh axis runs over, the one named last changes fastest.
Arguments:
- k_cache: bfloat16 [256, 256, 512], P(('request', 'mirror'), None, 'tensor'), parts along dimension 0, may hold values from -12 to 12
- value_cache: bfloat16 [256, 256, 512], P(('request', 'mirror'), None, 'tensor'), parts along dimension 0, may hold values from -6 to 6
- recomputed_queries: bfloat16 [256, 128, 4096], P(('request', 'mirror'), None, 'tensor'), parts along dimension 0, may hold values from -36 to 36
- recomputed_keys: bfloat16 [256, 128, 512], P(('request', 'mirror'), None, 'tensor'), parts along dimension 0, may hold values from -6 to 6
- recomputed_values: bfloat16 [256, 128, 512], P(('request', 'mirror'), None, 'tensor'), parts along dimension 0, may hold values from -6 to 6
- sel_index: int32 [256, 128], P('request'), parts along dimension 0, may hold values from 0 to 255, as said below
- counts: int32 [256], P('request'), parts along dimension 0, may hold values from 48 to 128
- span_order: int32 [256], P('request'), parts along dimension 0, may hold values from 0 to 31, each once
Outputs:
- attn_out: bfloat16 [256, 128, 4096], P(('request', 'mirror'), None, 'tensor'), parts along dimension 0
- mixed_keys: bfloat16 [256, 256, 512], P(('request', 'mirror'), None, 'tensor'), parts along dimension 0
- mixed_values: bfloat16 [256, 256, 512], P(('request', 'mirror'), None, 'tensor'), parts along dimension 0
- deviation: float32 [256, 128], P(('request', 'mirror')), parts along dimension 0
The draws below stay inside these ranges and needn't reach their ends.
There are 8 independent parts, one for each index of `request`. The reference program is written for one: setup_inputs(seed, part) draws one part's arguments, and reference() takes and returns one part's arrays. A program takes and returns all parts, laid end to end along the dimension named above; each array names one. Nothing has to cross between parts.
Inputs may be any that keep to these rules, and one draw needn't show every extreme that they name: `sel_index`: for slot s the first counts[s] entries are distinct increasing token positions of span span_order[s]; the other entries are 0. `span_order`: a permutation of the span numbers.
All inputs are finite; a program needn't handle non-finite values.
Results may differ from the reference program's by a relative error of at most 0.0085.
Values may be sent and summed in bfloat16 or wider, within the bound.
A program may use at most 64 MiB of HBM per device.

```python
import math
import jax
import jax.numpy as jnp
from jax import lax

QUERY_HEADS = 32
KEY_VALUE_HEADS = 4
HEAD_DIMENSION = 128
SPAN_TOKENS = 256
SELECTED_SLOTS = 128
SPAN_NUMBER = 32


def row_counts(key):
    key = jax.random.fold_in(key, 101)
    first_key, second_key, third_key = jax.random.split(key, 3)
    least = 3 * SELECTED_SLOTS // 8
    drawn = jax.random.randint(first_key, (SPAN_NUMBER,), least, SELECTED_SLOTS + 1)
    low_at = jax.random.randint(second_key, (), 0, SPAN_NUMBER)
    high_at = (low_at + 1 + jax.random.randint(third_key, (), 0, SPAN_NUMBER - 1)) % SPAN_NUMBER
    return drawn.at[low_at].set(least).at[high_at].set(SELECTED_SLOTS)


def draw_counts(key, part):
    drawn = row_counts(key)
    return drawn.astype(jnp.int32)


def draw_sel_index(key, part):
    live_counts = row_counts(key)
    key = jax.random.fold_in(key, 11)
    row_keys = jax.random.split(key, SPAN_NUMBER)
    shuffled = jax.vmap(lambda one_key: jax.random.permutation(one_key, SPAN_TOKENS))(row_keys)[:, :SELECTED_SLOTS]
    ranks = jnp.arange(SELECTED_SLOTS, dtype=jnp.int32)[None, :]
    marked = jnp.where(ranks < live_counts[:, None], shuffled, SPAN_TOKENS)
    ordered = jnp.sort(marked, axis=1)
    return jnp.where(ordered >= SPAN_TOKENS, 0, ordered).astype(jnp.int32)


def draw_k_cache(key, part):
    key = jax.random.fold_in(key, 13)
    base_offset = jnp.clip(jax.random.normal(key, (SPAN_NUMBER, SPAN_TOKENS, KEY_VALUE_HEADS * HEAD_DIMENSION), jnp.float32), -6.0, 6.0)
    return base_offset.astype(jnp.bfloat16)


def draw_recomputed_queries(key, part):
    key = jax.random.fold_in(key, 17)
    base_offset = jnp.clip(jax.random.normal(key, (SPAN_NUMBER, SELECTED_SLOTS, QUERY_HEADS * HEAD_DIMENSION), jnp.float32), -6.0, 6.0)
    return base_offset.astype(jnp.bfloat16)


def levels(rng, extent, cuts, low, high):
    def one(dim, parts):
        draws = jax.random.uniform(jax.random.fold_in(jax.random.fold_in(rng, 6), dim), (parts,), jnp.float32, low / len(cuts), high / len(cuts))
        return jnp.repeat(jnp.exp(draws), extent[dim] // parts).reshape((-1,) + (1,) * (len(extent) - dim - 1))

    level = one(*cuts[0])
    for cut in cuts[1:]:
        level = level * one(*cut)
    return level


def scatter_about(stream_key, shape, scale, reach, shards=(), kind=jnp.bfloat16):
    values = jax.random.normal(stream_key, shape, jnp.float32) * scale
    if len(shards) > 0:
        values = levels(stream_key, shape, shards, -0.22, 0.18) * values
    return jnp.clip(values, min=-reach, max=reach).astype(kind)


def setup_inputs(seed: int = 0, part: int = 0) -> dict:
    arg_keys = jax.random.split(jax.random.key(seed), 9)
    own_keys = jax.random.split(jax.random.fold_in(arg_keys[8], part), 9)
    return {
        "k_cache": draw_k_cache(jax.random.fold_in(jax.random.fold_in(arg_keys[8], part), 71), part),
        "value_cache": scatter_about(own_keys[1], (SPAN_NUMBER, SPAN_TOKENS, KEY_VALUE_HEADS * HEAD_DIMENSION), 1.0, 6.0, ((0, 32), (2, 2))),
        "recomputed_queries": draw_recomputed_queries(jax.random.fold_in(jax.random.fold_in(arg_keys[8], part), 71), part),
        "recomputed_keys": scatter_about(own_keys[3], (SPAN_NUMBER, SELECTED_SLOTS, KEY_VALUE_HEADS * HEAD_DIMENSION), 1.0, 6.0, ((0, 32), (2, 2))),
        "recomputed_values": scatter_about(own_keys[4], (SPAN_NUMBER, SELECTED_SLOTS, KEY_VALUE_HEADS * HEAD_DIMENSION), 1.0, 6.0, ((0, 32), (2, 2))),
        "sel_index": draw_sel_index(jax.random.fold_in(jax.random.fold_in(arg_keys[8], part), 71), part),
        "counts": draw_counts(jax.random.fold_in(jax.random.fold_in(arg_keys[8], part), 71), part),
        "span_order": jax.random.permutation(own_keys[7], SPAN_NUMBER).astype(jnp.int32),
    }


large_negative = -1e+30

def absorb(carry_state, query_block, key_row_block, value_row_block, allowed, needed, scaling):

    def update(current):
        highest, totals, summed = current
        scores = jnp.einsum('rhgd,khd->hgrk', query_block.astype(jnp.float32), key_row_block.astype(jnp.float32)) * scaling
        scores = jnp.where(allowed, scores, large_negative)
        new_high = jnp.maximum(highest, lax.optimization_barrier(jnp.max(scores, axis=-1)))
        weights = jnp.where(allowed, jnp.exp(scores - new_high[..., None]), 0.0)
        decay_factor = jnp.exp(highest - new_high)
        totals = totals * decay_factor + lax.optimization_barrier(jnp.sum(weights, axis=-1))
        rounded = lax.optimization_barrier(weights.astype(jnp.bfloat16)).astype(jnp.float32)
        summed = summed * decay_factor[..., None] + jnp.einsum('hgrk,khd->hgrd', rounded, value_row_block.astype(jnp.float32))
        return (new_high, totals, summed)
    return lax.cond(needed, update, lambda current: current, carry_state)

def reference(k_cache, value_cache, recomputed_queries, recomputed_keys, recomputed_values, sel_index, counts, span_order):
    query_group_width = QUERY_HEADS // KEY_VALUE_HEADS
    scaling = 1.0 / math.sqrt(HEAD_DIMENSION)
    slot_range = jnp.arange(SPAN_NUMBER, dtype=jnp.int32)
    slot_of = lax.optimization_barrier(jnp.sum(slot_range[:, None] * (span_order[:, None] == slot_range[None, :]).astype(jnp.int32), axis=0))
    live_table = jnp.arange(SELECTED_SLOTS, dtype=jnp.int32)[None, :] < counts[:, None]
    rows_by_span = sel_index[slot_of]
    live_by_span = live_table[slot_of]
    fresh_keys = recomputed_keys[slot_of]
    fresh_values = recomputed_values[slot_of]
    places = jnp.arange(SPAN_TOKENS, dtype=jnp.int32)
    matched = (places[None, :, None] == rows_by_span[:, None, :]) & live_by_span[:, None, :]
    markers = matched.astype(jnp.float32)
    any_hit = jnp.any(matched, axis=2)[..., None]
    moved_keys = jnp.einsum('cus,csf->cuf', markers, fresh_keys.astype(jnp.float32)).astype(jnp.bfloat16)
    moved_values = jnp.einsum('cus,csf->cuf', markers, fresh_values.astype(jnp.float32)).astype(jnp.bfloat16)
    mixed_keys = jnp.where(any_hit, moved_keys, k_cache)
    mixed_values = jnp.where(any_hit, moved_values, value_cache)
    old_rows = jnp.einsum('cus,cuf->csf', markers, k_cache.astype(jnp.float32))
    gap = fresh_keys.astype(jnp.float32) - old_rows
    deviation = jnp.where(live_by_span, lax.optimization_barrier(jnp.mean(gap * gap, axis=-1)), 0.0)

    def one_slot(slot_number):
        query_block = recomputed_queries[slot_number].reshape(SELECTED_SLOTS, KEY_VALUE_HEADS, query_group_width, HEAD_DIMENSION)
        query_tokens = sel_index[slot_number]
        initial_state = (jnp.full((KEY_VALUE_HEADS, query_group_width, SELECTED_SLOTS), large_negative, jnp.float32), jnp.zeros((KEY_VALUE_HEADS, query_group_width, SELECTED_SLOTS), jnp.float32), jnp.zeros((KEY_VALUE_HEADS, query_group_width, SELECTED_SLOTS, HEAD_DIMENSION), jnp.float32))

        def step(carry_state, other_slot):
            span_number = span_order[other_slot]
            key_row_block = mixed_keys[span_number].reshape(SPAN_TOKENS, KEY_VALUE_HEADS, HEAD_DIMENSION)
            value_row_block = mixed_values[span_number].reshape(SPAN_TOKENS, KEY_VALUE_HEADS, HEAD_DIMENSION)
            allowed = (other_slot < slot_number) | (places[None, :] <= query_tokens[:, None])
            return (absorb(carry_state, query_block, key_row_block, value_row_block, allowed, other_slot <= slot_number, scaling), None)
        final_state, _ = lax.scan(step, initial_state, slot_range)
        highest, totals, summed = final_state
        result = (summed / totals[..., None]).transpose(2, 0, 1, 3).reshape(SELECTED_SLOTS, QUERY_HEADS * HEAD_DIMENSION)
        return jnp.where(live_table[slot_number][:, None], result, 0.0).astype(jnp.bfloat16)
    attn_out = lax.map(one_slot, slot_range)
    return (attn_out, mixed_keys, mixed_values, deviation)
```

```python
import functools
import math

import jax
import jax.numpy as jnp
from jax import lax
from jax.experimental import pallas as pl
from jax.experimental.pallas import tpu as pltpu
from jax.sharding import PartitionSpec as P

HEAD = 128
TOKENS = 256
ROWS = 128
LEAST = 48
KEPT = TOKENS - LEAST
PART = KEPT + ROWS
PAD = 384
GROUP = 8
TILE = 256
LOW = -1e30
FAR = 1e9
SCALE = math.log2(math.e) / math.sqrt(HEAD)
F32 = jnp.float32
BF16 = jnp.bfloat16


def dot(a, b):
    return jnp.dot(a, b, preferred_element_type=F32)


def dot_nt(a, b):
    return lax.dot_general(a, b, (((1,), (1,)), ((), ())), preferred_element_type=F32)


def iota(shape, dim):
    return lax.broadcasted_iota(jnp.int32, shape, dim).astype(F32)


def turn(row):
    return jnp.broadcast_to(row, (ROWS, ROWS)).T


def kept_rows(sel_row, live):
    places = iota((ROWS, TOKENS), 1)
    side = turn(sel_row)
    side = jnp.concatenate([side, side], axis=1)
    slots = iota((ROWS, TOKENS), 0)
    hits = jnp.where((places == side) & (slots < live), 1.0, 0.0)
    keep = 1.0 - jnp.max(hits, axis=0, keepdims=True)
    before = jnp.where(iota((TOKENS, TOKENS), 0) < iota((TOKENS, TOKENS), 1), 1.0, 0.0)
    rank = dot(jnp.broadcast_to(keep, (8, TOKENS)).astype(BF16), before.astype(BF16))[:1]
    rank = jnp.where(keep > 0.5, rank, -1.0)
    return jnp.where(iota((PAD, TOKENS), 0) == rank, 1.0, 0.0).astype(BF16)


def kernel(
    levels,
    order_s,
    counts_s,
    k_ref,
    v_ref,
    q_ref,
    rk_ref,
    rv_ref,
    sel_ref,
    counts_ref,
    order_ref,
    out_ref,
    mk_ref,
    mv_ref,
    dev_ref,
    blocks,
    queries,
    acc,
    total,
    top,
    token_of,
    limit,
    away,
    rows_out,
    rows_in,
    answer,
    gap_mine,
    gap_other,
    block_recv,
    ring_send,
    away_send,
    query_send,
    query_recv,
    rows_send,
    rows_recv,
    answer_send,
    answer_recv,
    gap_send,
    gap_recv,
):
    spans = 2 * levels
    half_way = levels // 2
    last = levels - 1
    me = lax.axis_index("mirror")
    core = lax.axis_index("tensor")
    z, y = me // 2, me % 2
    partner = z * 2 + 1 - y
    up = ((z + 1) % levels) * 2 + y
    down = ((z + levels - 1) % levels) * 2 + y
    mine_at = pl.multiple_of(y * HEAD, HEAD)
    away_at = pl.multiple_of((1 - y) * HEAD, HEAD)
    mine_q = y * GROUP * HEAD
    away_q = (1 - y) * GROUP * HEAD

    barrier = pltpu.get_barrier_semaphore()
    for other in (up, down, partner):
        pl.semaphore_signal(barrier, inc=1, device_id={"mirror": other})
    pl.semaphore_signal(barrier, inc=1, device_id={"tensor": 1 - core})

    def send(src, dst, send_sem, recv_sem, to):
        return pltpu.make_async_remote_copy(
            src_ref=src, dst_ref=dst, send_sem=send_sem, recv_sem=recv_sem, device_id=to
        )

    def part(unit, kv, slot):
        return blocks.at[unit, kv, slot, pl.ds(0, PART), :]

    def ring(direction, src, unit, kv, slot, tag):
        to = {"mirror": up if direction == 0 else down}
        return send(
            src, part(unit, kv, slot), ring_send.at[direction, unit, tag],
            block_recv.at[unit, kv, slot], to,
        )

    def arrived(unit, kv, slot):
        send(
            part(unit, kv, slot), part(unit, kv, slot), ring_send.at[0, 0, 0],
            block_recv.at[unit, kv, slot], {"mirror": up},
        ).wait_recv()

    def find(s, found):
        return jnp.where(order_s[s] == me, s, found)

    my_slot = lax.fori_loop(0, spans, find, 0)
    my_live = counts_s[my_slot].astype(F32)
    sel_all = sel_ref[...].astype(F32)
    chosen = jnp.where(order_ref[...] == me, 1.0, 0.0)
    my_sel = dot(jnp.broadcast_to(chosen, (8, spans)).astype(BF16), sel_all.astype(BF16))[:1]

    keep_mine = kept_rows(my_sel, my_live)[:KEPT]
    for kv, (cache, fresh) in enumerate(((k_ref, rk_ref), (v_ref, rv_ref))):
        packed = dot(keep_mine, cache[:, pl.ds(mine_at, HEAD)]).astype(BF16)
        blocks[0, kv, 0, 0:KEPT, :] = packed
        blocks[0, kv, 0, KEPT:PART, :] = fresh[:, pl.ds(mine_at, HEAD)]
        packed = dot(keep_mine, cache[:, pl.ds(away_at, HEAD)]).astype(BF16)
        away[kv, 0:KEPT, :] = packed
        away[kv, KEPT:PART, :] = fresh[:, pl.ds(away_at, HEAD)]

    pl.semaphore_wait(barrier, 4)

    def across(kv):
        return send(
            away.at[kv], part(0, kv, 1), away_send.at[kv], block_recv.at[0, kv, 1],
            {"mirror": partner},
        )

    def ask(g):
        return send(
            q_ref.at[:, pl.ds(pl.multiple_of(away_q + g * HEAD, HEAD), HEAD)],
            queries.at[1, pl.ds(g * ROWS, ROWS), :],
            query_send.at[g], query_recv.at[g], {"mirror": partner},
        )

    for kv in range(2):
        across(kv).start()
        for direction in range(2):
            ring(direction, part(0, kv, 0), 1, kv, direction, kv).start()
    for g in range(GROUP):
        ask(g).start()

    counts_f = counts_ref[...].astype(F32)
    c_at, s_at = iota((spans, spans), 0), iota((spans, spans), 1)
    pick = order_ref[...].astype(F32) == c_at
    slot_of = jnp.sum(jnp.where(pick, s_at, 0.0), axis=1, keepdims=True)
    slot_live = jnp.sum(jnp.where(pick, counts_f, 0.0), axis=1, keepdims=True)
    row_live = jnp.sum(jnp.where(c_at == s_at, counts_f, 0.0), axis=1, keepdims=True)
    span_at = iota((spans, PAD), 0)[:, :1]
    lane = iota((spans, PAD), 1)
    for o, slot in ((0, me), (1, partner)):
        at = slot.astype(F32)
        live = counts_s[slot].astype(F32)
        sel_row = sel_ref[pl.ds(slot, 1), :].astype(F32)
        limit[o] = turn(sel_row)
        sel_8 = jnp.broadcast_to(sel_row, (8, ROWS)).astype(BF16)
        shift = jnp.where(iota((PAD, ROWS), 0) - KEPT == iota((PAD, ROWS), 1), 1.0, 0.0)
        places = iota((8, TOKENS), 1).astype(BF16)
        diagonal = dot_nt(places, kept_rows(sel_row, live)) + dot_nt(sel_8, shift.astype(BF16))
        diagonal = jnp.broadcast_to(diagonal[:1], (spans, PAD))
        end_kept = jnp.where(slot_of <= at, jnp.minimum(TOKENS - slot_live, float(KEPT)), 0.0)
        end_rows = jnp.where(span_at <= at, KEPT + row_live, 0.0)
        same_kept = jnp.where(slot_of == at, 1.0, 0.0)
        same_rows = jnp.where(span_at == at, 1.0, 0.0)
        is_kept = lane < KEPT
        valid = lane < jnp.where(is_kept, end_kept, end_rows)
        same = jnp.where(is_kept, same_kept, same_rows)
        token_of[o] = jnp.where(valid, same * diagonal, FAR)

    for g in range(GROUP):
        queries[0, g * ROWS:(g + 1) * ROWS, :] = q_ref[
            :, pl.ds(pl.multiple_of(mine_q + g * HEAD, HEAD), HEAD)
        ]
    acc[...] = jnp.zeros_like(acc)
    total[...] = jnp.zeros_like(total)
    top[...] = jnp.full_like(top, LOW)
    blocks[:, :, :, PART:PAD, :] = jnp.zeros((levels, 2, 2, PAD - PART, HEAD), BF16)

    for kv in range(2):
        arrived(0, kv, 1)
        for direction in range(2):
            ring(direction, part(0, kv, 1), 2, kv, direction, kv).start()
    for g in range(GROUP):
        ask(g).wait_recv()

    def absorb(unit):
        distance = (unit + 1) // 2
        half = jnp.where(unit == 0, 0, (unit + 1) % 2)
        column = (y + half) % 2
        whole = (unit == 0) | (unit == last)
        first = ((z + levels - distance) % levels) * 2 + jnp.where(whole, y, column)
        second = ((z + distance) % levels) * 2 + jnp.where(whole, 1 - y, column)
        keys = blocks[unit, 0].reshape(2 * PAD, HEAD)
        values = blocks[unit, 1].reshape(2 * PAD, HEAD)
        values = jnp.concatenate([values, jnp.ones_like(values)], axis=1)
        for o in (1, 0):
            tokens = jnp.concatenate(
                [token_of[o, pl.ds(first, 1), :], token_of[o, pl.ds(second, 1), :]], axis=1
            )
            bound = limit[o]
            seen = jnp.concatenate(
                [tokens[:, j:j + 128] <= bound for j in range(0, 2 * PAD, 128)], axis=1
            )
            for t in range(GROUP * ROWS // TILE):
                rows = slice(t * TILE, (t + 1) * TILE)
                scores = dot_nt(queries[o, rows, :], keys) * SCALE
                scores = scores.reshape(TILE // ROWS, ROWS, 2 * PAD)
                scores = jnp.where(seen[None], scores, LOW).reshape(TILE, 2 * PAD)
                old = top[o, rows, :]
                new = jnp.maximum(old, jnp.max(scores, axis=1, keepdims=True))
                top[o, rows, :] = new
                decay = jnp.exp2(old - new)
                weights = jnp.exp2(scores - jnp.concatenate([new] * (2 * PAD // 128), axis=1))
                found = dot(weights.astype(BF16), values)
                total[o, rows, :] = total[o, rows, :] * decay + found[:, HEAD:]
                acc[o, rows, :] = acc[o, rows, :] * decay + found[:, :HEAD]

    def step(unit, carry):
        @pl.when((unit >= 1) & (unit < last))
        def _():
            for kv in range(2):
                for direction in range(2):
                    arrived(unit, kv, direction)

                    @pl.when(unit < last - 2)
                    def _():
                        ring(
                            direction, part(unit, kv, direction), unit + 2, kv, direction, kv
                        ).start()

                    if kv == direction:
                        @pl.when(unit >= last - 2)
                        def _():
                            half = (unit + 1) % 2
                            ring(
                                direction, part(unit, kv, direction), last, kv, half, half
                            ).start()

        @pl.when(unit == last)
        def _():
            for half in range(2):
                for kv in range(2):
                    arrived(last, kv, half)

        absorb(unit)
        return carry

    lax.fori_loop(0, levels, step, 0)

    def finish(o, g, live):
        rows = slice(g * ROWS, (g + 1) * ROWS)
        result = acc[o, rows, :] / total[o, rows, :]
        return jnp.where(iota((ROWS, HEAD), 0) < live, result, 0.0).astype(BF16)

    def reply(g):
        return send(
            answer.at[g],
            out_ref.at[:, pl.ds(pl.multiple_of(mine_q + g * HEAD, HEAD), HEAD)],
            answer_send.at[g], answer_recv.at[g], {"mirror": partner},
        )

    partner_live = counts_s[partner].astype(F32)
    for g in range(GROUP):
        answer[g] = finish(1, g, partner_live)
        reply(g).start()

    def where_is(slot):
        half = (slot + y) % 2
        ahead = (slot // 2 + levels - z) % levels
        distance = jnp.minimum(ahead, levels - ahead)
        whole = (ahead == 0) | (ahead == half_way)
        unit = jnp.where(ahead == 0, 0, jnp.where(ahead == half_way, last, 2 * distance - 1 + half))
        side = jnp.where(whole, half, jnp.where(ahead < half_way, 1, 0))
        return unit, side

    def find_partner(s, found):
        return jnp.where(order_s[s] == partner, s, found)

    partner_slot = lax.fori_loop(0, spans, find_partner, 0)
    unit, side = where_is(partner_slot)
    for kv in range(2):
        rows_out[kv] = blocks[unit, kv, side, KEPT:PART, :]
    hand = send(rows_out, rows_in, rows_send, rows_recv, {"mirror": partner})
    hand.start()

    own_live = counts_s[me].astype(F32)
    for g in range(GROUP):
        out_ref[:, pl.ds(pl.multiple_of(mine_q + g * HEAD, HEAD), HEAD)] = finish(0, g, own_live)

    unit, side = where_is(my_slot)
    match = (iota((TOKENS, ROWS), 0) == my_sel) & (iota((TOKENS, ROWS), 1) < my_live)
    markers = jnp.where(match, 1.0, 0.0)
    hit = jnp.max(markers, axis=1, keepdims=True)
    markers = markers.astype(BF16)
    side_sel = turn(my_sel)
    side_sel = jnp.concatenate([side_sel, side_sel], axis=1)
    match = (iota((ROWS, TOKENS), 1) == side_sel) & (iota((ROWS, TOKENS), 0) < my_live)
    markers_t = jnp.where(match, 1.0, 0.0).astype(BF16)

    def blend(fresh, cache, result, at):
        moved = dot(markers, fresh)
        old = cache[:, pl.ds(at, HEAD)]
        result[:, pl.ds(at, HEAD)] = jnp.where(hit > 0.5, moved, old.astype(F32)).astype(BF16)

    def gaps(fresh, at):
        gap = fresh.astype(F32) - dot(markers_t, k_ref[:, pl.ds(at, HEAD)])
        return jnp.sum(gap * gap, axis=1, keepdims=True)

    fresh_k = blocks[unit, 0, side, KEPT:PART, :]
    fresh_v = blocks[unit, 1, side, KEPT:PART, :]
    blend(fresh_k, k_ref, mk_ref, mine_at)
    blend(fresh_v, v_ref, mv_ref, mine_at)
    squares = gaps(fresh_k, mine_at)
    hand.wait_recv()
    blend(rows_in[0], k_ref, mk_ref, away_at)
    blend(rows_in[1], v_ref, mv_ref, away_at)
    squares = squares + gaps(rows_in[0], away_at)
    gap_mine[...] = jnp.broadcast_to(squares, (ROWS, ROWS)).T[:8]
    swap = send(gap_mine, gap_other, gap_send, gap_recv, {"tensor": 1 - core})
    swap.start()
    swap.wait_recv()
    mean = (gap_mine[:1] + gap_other[:1]) / (4.0 * HEAD)
    dev_ref[...] = jnp.where(iota((1, ROWS), 1) < my_live, mean, 0.0)

    for g in range(GROUP):
        reply(g).wait_recv()

    swap.wait_send()
    hand.wait_send()
    for g in range(GROUP):
        reply(g).wait_send()
        ask(g).wait_send()
    for kv in range(2):
        across(kv).wait_send()

    def drain(unit, carry):
        for direction in range(2):
            for kv in range(2):
                ring(direction, part(0, 0, 0), unit, kv, 0, kv).wait_send()
        return carry

    lax.fori_loop(1, levels, drain, 0)


def body(k_cache, value_cache, queries, new_keys, new_values, sel_index, counts, span_order):
    spans = sel_index.shape[0]
    levels = spans // 2
    columns = queries.shape[2]
    wide = k_cache.shape[2]
    smem = pl.BlockSpec(memory_space=pltpu.SMEM)
    vmem = pl.BlockSpec(memory_space=pltpu.VMEM)
    dma = pltpu.SemaphoreType.DMA
    stats = pltpu.VMEM((2, GROUP * ROWS, HEAD), F32)
    out, mk, mv, dev = pl.pallas_call(
        functools.partial(kernel, levels),
        out_shape=(
            jax.ShapeDtypeStruct((ROWS, columns), BF16),
            jax.ShapeDtypeStruct((TOKENS, wide), BF16),
            jax.ShapeDtypeStruct((TOKENS, wide), BF16),
            jax.ShapeDtypeStruct((1, ROWS), F32),
        ),
        in_specs=[smem, smem] + [vmem] * 8,
        out_specs=(vmem,) * 4,
        scratch_shapes=[
            pltpu.VMEM((levels, 2, 2, PAD, HEAD), BF16),
            pltpu.VMEM((2, GROUP * ROWS, HEAD), BF16),
            stats,
            stats,
            stats,
            pltpu.VMEM((2, spans, PAD), F32),
            pltpu.VMEM((2, ROWS, ROWS), F32),
            pltpu.VMEM((2, PART, HEAD), BF16),
            pltpu.VMEM((2, ROWS, HEAD), BF16),
            pltpu.VMEM((2, ROWS, HEAD), BF16),
            pltpu.VMEM((GROUP, ROWS, HEAD), BF16),
            pltpu.VMEM((8, ROWS), F32),
            pltpu.VMEM((8, ROWS), F32),
            dma((levels, 2, 2)),
            dma((2, levels, 2)),
            dma((2,)),
            dma((GROUP,)),
            dma((GROUP,)),
            dma,
            dma,
            dma((GROUP,)),
            dma((GROUP,)),
            dma,
            dma,
        ],
        compiler_params=pltpu.CompilerParams(
            collective_id=0, has_side_effects=True, vmem_limit_bytes=48 * 2**20
        ),
    )(
        span_order,
        counts,
        k_cache[0],
        value_cache[0],
        queries[0],
        new_keys[0],
        new_values[0],
        sel_index,
        counts[None],
        span_order[None],
    )
    return out[None], mk[None], mv[None], dev


def solution(mesh):
    whole = P(("request", "mirror"), None, "tensor")
    in_specs = (whole,) * 5 + (P("request", None), P("request"), P("request"))
    out_specs = (whole, whole, whole, P(("request", "mirror"), None))
    return jax.shard_map(body, mesh=mesh, in_specs=in_specs, out_specs=out_specs, check_vma=False)
```

```python
import functools
import math

import jax
import jax.numpy as jnp
from jax import lax
from jax.experimental import pallas as pl
from jax.experimental.pallas import tpu as pltpu
from jax.sharding import PartitionSpec as P

HEAD = 128
TOKENS = 256
ROWS = 128
LEAST = 48
KEPT = TOKENS - LEAST
GROUP = 8
TILE = 256
LOW = -1e30
FAR = 1e9
SCALE = math.log2(math.e) / math.sqrt(HEAD)
F32 = jnp.float32
BF16 = jnp.bfloat16


def dot(a, b):
    return jnp.dot(a, b, preferred_element_type=F32)


def dot_nt(a, b):
    return lax.dot_general(a, b, (((1,), (1,)), ((), ())), preferred_element_type=F32)


def iota(shape, dim):
    return lax.broadcasted_iota(jnp.int32, shape, dim).astype(F32)


def turn(row):
    return jnp.broadcast_to(row, (ROWS, ROWS)).T


def kept_rows(sel_row, live):
    places = iota((ROWS, TOKENS), 1)
    side = turn(sel_row)
    side = jnp.concatenate([side, side], axis=1)
    slots = iota((ROWS, TOKENS), 0)
    hits = jnp.where((places == side) & (slots < live), 1.0, 0.0)
    keep = 1.0 - jnp.max(hits, axis=0, keepdims=True)
    before = jnp.where(iota((TOKENS, TOKENS), 0) < iota((TOKENS, TOKENS), 1), 1.0, 0.0)
    rank = dot(jnp.broadcast_to(keep, (8, TOKENS)).astype(BF16), before.astype(BF16))[:1]
    rank = jnp.where(keep > 0.5, rank, -1.0)
    return jnp.where(iota((TOKENS, TOKENS), 0) == rank, 1.0, 0.0).astype(BF16)


def kernel(
    levels,
    order_h,
    counts_h,
    sel_h,
    k_h,
    v_h,
    q_h,
    rk_h,
    rv_h,
    out_ref,
    mk_ref,
    mv_ref,
    dev_ref,
    order_s,
    counts_s,
    order_v,
    counts_v,
    sel_ref,
    k_ref,
    v_ref,
    kept,
    fresh,
    queries,
    acc,
    total,
    top,
    token_kept,
    token_fresh,
    limit,
    away,
    rows_out,
    rows_in,
    answer,
    gap_mine,
    gap_other,
    load_sem,
    query_load,
    block_recv,
    far_recv,
    ring_send,
    far_send,
    away_send,
    query_send,
    query_recv,
    rows_send,
    rows_recv,
    answer_send,
    answer_recv,
    gap_send,
    gap_recv,
):
    spans = 2 * levels
    half_way = levels // 2
    last = levels - 1
    me = lax.axis_index("mirror")
    core = lax.axis_index("tensor")
    z, y = me // 2, me % 2
    partner = z * 2 + 1 - y
    up = ((z + 1) % levels) * 2 + y
    down = ((z + levels - 1) % levels) * 2 + y
    mine_at = pl.multiple_of(y * HEAD, HEAD)
    away_at = pl.multiple_of((1 - y) * HEAD, HEAD)
    mine_q = y * GROUP * HEAD
    away_q = (1 - y) * GROUP * HEAD

    barrier = pltpu.get_barrier_semaphore()
    for other in (up, down, partner):
        pl.semaphore_signal(barrier, inc=1, device_id={"mirror": other})
    pl.semaphore_signal(barrier, inc=1, device_id={"tensor": 1 - core})

    def q_columns(at, g):
        return q_h.at[:, pl.ds(pl.multiple_of(at + g * HEAD, HEAD), HEAD)]

    loads = [
        pltpu.make_async_copy(src, dst, load_sem.at[i])
        for i, (src, dst) in enumerate(
            (
                (order_h, order_s),
                (counts_h, counts_s),
                (order_h, order_v),
                (counts_h, counts_v),
                (sel_h, sel_ref),
                (k_h, k_ref),
                (v_h, v_ref),
                (rk_h.at[:, pl.ds(mine_at, HEAD)], fresh.at[0, 0, 0]),
                (rv_h.at[:, pl.ds(mine_at, HEAD)], fresh.at[0, 1, 0]),
            )
        )
    ]
    for load in loads:
        load.start()

    def load_query(g):
        return pltpu.make_async_copy(
            q_columns(mine_q, g), queries.at[0, pl.ds(g * ROWS, ROWS), :], query_load.at[g]
        )

    for g in range(GROUP):
        load_query(g).start()

    def send(src, dst, send_sem, recv_sem, to):
        return pltpu.make_async_remote_copy(
            src_ref=src, dst_ref=dst, send_sem=send_sem, recv_sem=recv_sem, device_id=to
        )

    def rows_of(unit, slot):
        return fresh.at[unit, :, slot]

    def kept_of(unit, slot):
        return kept.at[unit, :, slot, pl.ds(0, KEPT), :]

    def way(direction):
        return {"mirror": up if direction == 0 else down}

    def ring(direction, unit, slot, kind, to_unit):
        piece = (rows_of, kept_of)[kind]
        return send(
            piece(unit, slot), piece(to_unit, direction), ring_send.at[direction, to_unit, kind],
            block_recv.at[to_unit, direction, kind], way(direction),
        )

    def far(kv, half, kind, unit):
        if kind == 0:
            src, dst = fresh.at[unit, kv, kv], fresh.at[last, kv, half]
        else:
            src = kept.at[unit, kv, kv, pl.ds(0, KEPT), :]
            dst = kept.at[last, kv, half, pl.ds(0, KEPT), :]
        return send(src, dst, far_send.at[kv, half, kind], far_recv.at[kv, half, kind], way(kv))

    def arrived(unit, slot, kind):
        piece = (rows_of, kept_of)[kind]
        send(
            piece(unit, slot), piece(unit, slot), ring_send.at[0, 0, 0],
            block_recv.at[unit, slot, kind], way(0),
        ).wait_recv()

    acc[...] = jnp.zeros_like(acc)
    total[...] = jnp.zeros_like(total)
    top[...] = jnp.full_like(top, LOW)
    kept[:, 1, :, KEPT:, :] = jnp.zeros((levels, 2, TOKENS - KEPT, HEAD), BF16)

    pl.semaphore_wait(barrier, 4)

    for kv, rows_h in enumerate((rk_h, rv_h)):
        send(
            rows_h.at[:, pl.ds(away_at, HEAD)], fresh.at[0, kv, 1], away_send.at[0],
            block_recv.at[0, 1, 0], {"mirror": partner},
        ).start()
        for direction in range(2):
            send(
                rows_h.at[:, pl.ds(mine_at, HEAD)], fresh.at[1, kv, direction],
                ring_send.at[direction, 1, 0], block_recv.at[1, direction, 0], way(direction),
            ).start()

    for load in loads:
        load.wait()

    def find(s, found):
        return jnp.where(order_s[0, s] == me, s, found)

    my_slot = lax.fori_loop(0, spans, find, 0)
    my_live = counts_s[0, my_slot].astype(F32)
    sel_all = sel_ref[...].astype(F32)
    chosen = jnp.where(order_v[...] == me, 1.0, 0.0)
    my_sel = dot(jnp.broadcast_to(chosen, (8, spans)).astype(BF16), sel_all.astype(BF16))[:1]

    keep_mine = kept_rows(my_sel, my_live)[:KEPT]
    for kv, cache in enumerate((k_ref, v_ref)):
        away[kv] = dot(keep_mine, cache[:, pl.ds(away_at, HEAD)]).astype(BF16)
    across = send(
        away, kept_of(0, 1), away_send.at[1], block_recv.at[0, 1, 1], {"mirror": partner}
    )
    across.start()
    for kv, cache in enumerate((k_ref, v_ref)):
        kept[0, kv, 0, 0:KEPT, :] = dot(keep_mine, cache[:, pl.ds(mine_at, HEAD)]).astype(BF16)
    for direction in range(2):
        ring(direction, 0, 0, 1, 1).start()

    def ask(g):
        return send(
            q_columns(away_q, g), queries.at[1, pl.ds(g * ROWS, ROWS), :],
            query_send.at[g], query_recv.at[g], {"mirror": partner},
        )

    for g in range(GROUP):
        ask(g).start()

    arrived(0, 1, 0)
    for direction in range(2):
        ring(direction, 0, 1, 0, 2).start()

    counts_f = counts_v[...].astype(F32)
    c_at, s_at = iota((spans, spans), 0), iota((spans, spans), 1)
    pick = order_v[...].astype(F32) == c_at
    slot_of = jnp.sum(jnp.where(pick, s_at, 0.0), axis=1, keepdims=True)
    slot_live = jnp.sum(jnp.where(pick, counts_f, 0.0), axis=1, keepdims=True)
    row_live = jnp.sum(jnp.where(c_at == s_at, counts_f, 0.0), axis=1, keepdims=True)
    span_at = iota((spans, ROWS), 0)[:, :1]
    for o, slot in ((0, me), (1, partner)):
        at = slot.astype(F32)
        live = counts_s[0, slot].astype(F32)
        sel_row = sel_ref[pl.ds(slot, 1), :].astype(F32)
        limit[o] = turn(sel_row)
        places = iota((8, TOKENS), 1).astype(BF16)
        diagonal = dot_nt(places, kept_rows(sel_row, live))[:1]
        end = jnp.where(slot_of <= at, jnp.minimum(TOKENS - slot_live, float(KEPT)), 0.0)
        same = jnp.where(slot_of == at, 1.0, 0.0)
        token_kept[o] = jnp.where(iota((spans, TOKENS), 1) < end, same * diagonal, FAR)
        end = jnp.where(span_at <= at, row_live, 0.0)
        same = jnp.where(span_at == at, 1.0, 0.0)
        token_fresh[o] = jnp.where(iota((spans, ROWS), 1) < end, same * sel_row, FAR)

    arrived(0, 1, 1)
    for direction in range(2):
        ring(direction, 0, 1, 1, 2).start()
    for g in range(GROUP):
        load_query(g).wait()
        ask(g).wait_recv()

    def attend(o, spans_at, keys, values, after=None):
        tokens = jnp.concatenate(
            [token_kept[o, pl.ds(c, 1), :] for c in spans_at]
            + [token_fresh[o, pl.ds(c, 1), :] for c in spans_at],
            axis=1,
        )
        wide = tokens.shape[1]
        split = keys[0].shape[0]
        bound = limit[o]
        seen = jnp.concatenate(
            [tokens[:, j:j + HEAD] <= bound for j in range(0, wide, HEAD)], axis=1
        )
        values = [jnp.concatenate([v, jnp.ones_like(v)], axis=1) for v in values]
        for t in range(GROUP * ROWS // TILE):
            rows = slice(t * TILE, (t + 1) * TILE)
            q = queries[o, rows, :]
            scores = jnp.concatenate([dot_nt(q, k) for k in keys], axis=1) * SCALE
            scores = scores.reshape(TILE // ROWS, ROWS, wide)
            scores = jnp.where(seen[None], scores, LOW).reshape(TILE, wide)
            old = top[o, rows, :]
            new = jnp.maximum(old, jnp.max(scores, axis=1, keepdims=True))
            decay = jnp.exp2(old - new)
            weights = jnp.exp2(scores - jnp.concatenate([new] * (wide // HEAD), axis=1))
            weights = weights.astype(BF16)
            found = dot(weights[:, :split], values[0]) + dot(weights[:, split:], values[1])
            sums = total[o, rows, :] * decay + found[:, HEAD:]
            mixed = acc[o, rows, :] * decay + found[:, :HEAD]
            if after is not None:
                after(t, mixed / sums)
            else:
                top[o, rows, :] = new
                total[o, rows, :] = sums
                acc[o, rows, :] = mixed

    def absorb(unit, o):
        distance = (unit + 1) // 2
        half = jnp.where(unit == 0, 0, (unit + 1) % 2)
        column = (y + half) % 2
        whole = (unit == 0) | (unit == last)
        first = ((z + levels - distance) % levels) * 2 + jnp.where(whole, y, column)
        second = ((z + distance) % levels) * 2 + jnp.where(whole, 1 - y, column)
        both = [
            (kept[unit, kv].reshape(2 * TOKENS, HEAD), fresh[unit, kv].reshape(2 * ROWS, HEAD))
            for kv in range(2)
        ]
        attend(o, (first, second), *both)

    def relay(unit):
        for kind in range(2):
            for direction in range(2):
                arrived(unit, direction, kind)

                @pl.when(unit < last - 2)
                def _():
                    ring(direction, unit, direction, kind, unit + 2).start()

                @pl.when(unit >= last - 2)
                def _():
                    far(direction, (unit + 1) % 2, kind, unit).start()

    def step(unit, carry):
        @pl.when(unit > 0)
        def _():
            relay(unit)

        for o in (1, 0):
            absorb(unit, o)
        return carry

    lax.fori_loop(0, last - 1, step, 0)
    relay(last - 1)
    absorb(last - 1, 1)

    def reply(g):
        return send(
            answer.at[g],
            out_ref.at[:, pl.ds(pl.multiple_of(mine_q + g * HEAD, HEAD), HEAD)],
            answer_send.at[g], answer_recv.at[g], {"mirror": partner},
        )

    def far_half(half, after=None):
        attend(
            1,
            (((z + half_way) % levels) * 2 + (y + half) % 2,),
            *[(kept[last, kv, half], fresh[last, kv, half]) for kv in range(2)],
            after=after,
        )

    def far_arrived(half, kind):
        for kv in range(2):
            far(kv, half, kind, last).wait_recv()

    far_arrived(0, 0)
    far_arrived(0, 1)
    far_half(0)
    far_arrived(1, 0)

    def where_is(slot):
        half = (slot + y) % 2
        ahead = (slot // 2 + levels - z) % levels
        distance = jnp.minimum(ahead, levels - ahead)
        whole = (ahead == 0) | (ahead == half_way)
        unit = jnp.where(ahead == 0, 0, jnp.where(ahead == half_way, last, 2 * distance - 1 + half))
        side = jnp.where(whole, half, jnp.where(ahead < half_way, 1, 0))
        return unit, side

    def find_partner(s, found):
        return jnp.where(order_s[0, s] == partner, s, found)

    partner_slot = lax.fori_loop(0, spans, find_partner, 0)
    unit, side = where_is(partner_slot)
    for kv in range(2):
        rows_out[kv] = fresh[unit, kv, side]
    hand = send(rows_out, rows_in, rows_send, rows_recv, {"mirror": partner})
    hand.start()

    far_arrived(1, 1)
    partner_live = counts_s[0, partner].astype(F32)
    own_live = counts_s[0, me].astype(F32)

    def live_only(result, live):
        return jnp.where(iota((ROWS, HEAD), 0) < live, result, 0.0).astype(BF16)

    def give_back(t, result):
        for i in range(TILE // ROWS):
            g = t * (TILE // ROWS) + i
            answer[g] = live_only(result[i * ROWS:(i + 1) * ROWS], partner_live)
            reply(g).start()

    far_half(1, give_back)

    unit, side = where_is(my_slot)
    match = (iota((TOKENS, ROWS), 0) == my_sel) & (iota((TOKENS, ROWS), 1) < my_live)
    markers = jnp.where(match, 1.0, 0.0)
    hit = jnp.max(markers, axis=1, keepdims=True)
    markers = markers.astype(BF16)
    side_sel = turn(my_sel)
    side_sel = jnp.concatenate([side_sel, side_sel], axis=1)
    match = (iota((ROWS, TOKENS), 1) == side_sel) & (iota((ROWS, TOKENS), 0) < my_live)
    markers_t = jnp.where(match, 1.0, 0.0).astype(BF16)

    def blend(new_rows, cache, result, at):
        moved = dot(markers, new_rows)
        old = cache[:, pl.ds(at, HEAD)]
        result[:, pl.ds(at, HEAD)] = jnp.where(hit > 0.5, moved, old.astype(F32)).astype(BF16)

    def gaps(new_rows, at):
        gap = new_rows.astype(F32) - dot(markers_t, k_ref[:, pl.ds(at, HEAD)])
        return jnp.sum(gap * gap, axis=1, keepdims=True)

    fresh_k = fresh[unit, 0, side]
    fresh_v = fresh[unit, 1, side]
    hand.wait_recv()
    squares = gaps(fresh_k, mine_at) + gaps(rows_in[0], away_at)
    gap_mine[...] = jnp.broadcast_to(squares, (ROWS, ROWS)).T[:8]
    swap = send(gap_mine, gap_other, gap_send, gap_recv, {"tensor": 1 - core})
    swap.start()
    blend(fresh_k, k_ref, mk_ref, mine_at)
    blend(fresh_v, v_ref, mv_ref, mine_at)
    blend(rows_in[0], k_ref, mk_ref, away_at)
    blend(rows_in[1], v_ref, mv_ref, away_at)

    def own_rest(unit, carry):
        absorb(unit, 0)
        return carry

    lax.fori_loop(last - 1, levels, own_rest, 0)
    for g in range(GROUP):
        rows = slice(g * ROWS, (g + 1) * ROWS)
        out_ref[:, pl.ds(pl.multiple_of(mine_q + g * HEAD, HEAD), HEAD)] = live_only(
            acc[0, rows, :] / total[0, rows, :], own_live
        )
    swap.wait_recv()
    mean = (gap_mine[:1] + gap_other[:1]) / (4.0 * HEAD)
    dev_ref[...] = jnp.where(iota((1, ROWS), 1) < my_live, mean, 0.0)

    swap.wait_send()
    hand.wait_send()
    across.wait_send()
    send(
        rows_of(0, 1), rows_of(0, 1), away_send.at[0], block_recv.at[0, 1, 0], way(0)
    ).wait_send()
    for kv in range(2):
        for half in range(2):
            for kind in range(2):
                far(kv, half, kind, last).wait_send()

    def drain(unit, carry):
        for direction in range(2):
            for kind in range(2):
                ring(direction, unit, direction, kind, unit).wait_send()
        return carry

    lax.fori_loop(1, last, drain, 0)
    for g in range(GROUP):
        ask(g).wait_send()
    for g in range(GROUP):
        reply(g).wait_recv()
        reply(g).wait_send()


def deliver(*refs):
    count = (len(refs) - 1) // 2
    sems = refs[-1]
    copies = [
        pltpu.make_async_copy(refs[i], refs[count + i], sems.at[i]) for i in range(count)
    ]
    for copy in copies:
        copy.start()
    for copy in copies:
        copy.wait()


def body(k_cache, value_cache, queries, new_keys, new_values, sel_index, counts, span_order):
    spans = sel_index.shape[0]
    levels = spans // 2
    columns = queries.shape[2]
    wide = k_cache.shape[2]
    hbm = pl.BlockSpec(memory_space=pltpu.HBM)
    vmem = pl.BlockSpec(memory_space=pltpu.VMEM)
    dma = pltpu.SemaphoreType.DMA
    stats = pltpu.VMEM((2, GROUP * ROWS, HEAD), F32)
    shapes = (
        jax.ShapeDtypeStruct((ROWS, columns), BF16),
        jax.ShapeDtypeStruct((TOKENS, wide), BF16),
        jax.ShapeDtypeStruct((TOKENS, wide), BF16),
        jax.ShapeDtypeStruct((1, ROWS), F32),
    )
    results = pl.pallas_call(
        functools.partial(kernel, levels),
        out_shape=shapes,
        in_specs=[hbm] * 8,
        out_specs=(vmem,) * 4,
        scratch_shapes=[
            pltpu.SMEM((1, spans), jnp.int32),
            pltpu.SMEM((1, spans), jnp.int32),
            pltpu.VMEM((1, spans), jnp.int32),
            pltpu.VMEM((1, spans), jnp.int32),
            pltpu.VMEM((spans, ROWS), jnp.int32),
            pltpu.VMEM((TOKENS, wide), BF16),
            pltpu.VMEM((TOKENS, wide), BF16),
            pltpu.VMEM((levels, 2, 2, TOKENS, HEAD), BF16),
            pltpu.VMEM((levels, 2, 2, ROWS, HEAD), BF16),
            pltpu.VMEM((2, GROUP * ROWS, HEAD), BF16),
            stats,
            stats,
            stats,
            pltpu.VMEM((2, spans, TOKENS), F32),
            pltpu.VMEM((2, spans, ROWS), F32),
            pltpu.VMEM((2, ROWS, ROWS), F32),
            pltpu.VMEM((2, KEPT, HEAD), BF16),
            pltpu.VMEM((2, ROWS, HEAD), BF16),
            pltpu.VMEM((2, ROWS, HEAD), BF16),
            pltpu.VMEM((GROUP, ROWS, HEAD), BF16),
            pltpu.VMEM((8, ROWS), F32),
            pltpu.VMEM((8, ROWS), F32),
            dma((9,)),
            dma((GROUP,)),
            dma((levels, 2, 2)),
            dma((2, 2, 2)),
            dma((2, levels, 2)),
            dma((2, 2, 2)),
            dma((2,)),
            dma((GROUP,)),
            dma((GROUP,)),
            dma,
            dma,
            dma((GROUP,)),
            dma((GROUP,)),
            dma,
            dma,
        ],
        compiler_params=pltpu.CompilerParams(
            collective_id=0, has_side_effects=True, vmem_limit_bytes=48 * 2**20
        ),
    )(
        span_order[None],
        counts[None],
        sel_index,
        k_cache[0],
        value_cache[0],
        queries[0],
        new_keys[0],
        new_values[0],
    )
    out, mk, mv, dev = pl.pallas_call(
        deliver,
        out_shape=shapes,
        in_specs=[vmem] * 4,
        out_specs=(hbm,) * 4,
        scratch_shapes=[dma((4,))],
    )(*results)
    return out[None], mk[None], mv[None], dev


def solution(mesh):
    whole = P(("request", "mirror"), None, "tensor")
    in_specs = (whole,) * 5 + (P("request", None), P("request"), P("request"))
    out_specs = (whole, whole, whole, P(("request", "mirror"), None))
    return jax.shard_map(body, mesh=mesh, in_specs=in_specs, out_specs=out_specs, check_vma=False)
```

```python
import functools
import math

import jax
import jax.numpy as jnp
from jax import lax
from jax.experimental import pallas as pl
from jax.experimental.pallas import tpu as pltpu
from jax.sharding import PartitionSpec as P

HEAD = 128
TOKENS = 256
ROWS = 128
LEAST = 48
KEPT = TOKENS - LEAST
GROUP = 8
VMEM_BYTES = 64 * 2**20 - 2**17
TILE = 256
LOW = -1e30
FAR = 1e9
SCALE = math.log2(math.e) / math.sqrt(HEAD)
F32 = jnp.float32
BF16 = jnp.bfloat16


def dot(a, b):
    return jnp.dot(a, b, preferred_element_type=F32)


def dot_nt(a, b):
    return lax.dot_general(a, b, (((1,), (1,)), ((), ())), preferred_element_type=F32)


def iota(shape, dim):
    return lax.broadcasted_iota(jnp.int32, shape, dim).astype(F32)


def turn(row):
    return jnp.broadcast_to(row, (ROWS, ROWS)).T


def kept_rows(sel_row, live):
    places = iota((ROWS, TOKENS), 1)
    side = turn(sel_row)
    side = jnp.concatenate([side, side], axis=1)
    slots = iota((ROWS, TOKENS), 0)
    hits = jnp.where((places == side) & (slots < live), 1.0, 0.0)
    keep = 1.0 - jnp.max(hits, axis=0, keepdims=True)
    before = jnp.where(iota((TOKENS, TOKENS), 0) < iota((TOKENS, TOKENS), 1), 1.0, 0.0)
    rank = dot(jnp.broadcast_to(keep, (8, TOKENS)).astype(BF16), before.astype(BF16))[:1]
    rank = jnp.where(keep > 0.5, rank, -1.0)
    return jnp.where(iota((TOKENS, TOKENS), 0) == rank, 1.0, 0.0).astype(BF16)


def kernel(
    levels,
    order_h,
    counts_h,
    sel_h,
    k_h,
    v_h,
    q_h,
    rk_h,
    rv_h,
    out_h,
    mk_h,
    mv_h,
    dev_h,
    mk_ref,
    mv_ref,
    dev_ref,
    order_s,
    counts_s,
    order_v,
    counts_v,
    sel_ref,
    k_ref,
    v_ref,
    kept,
    fresh,
    queries,
    acc,
    total,
    top,
    token_kept,
    token_fresh,
    limit,
    away,
    rows_out,
    rows_in,
    answer,
    own_out,
    gap_mine,
    gap_other,
    load_sem,
    store_sem,
    own_sem,
    query_load,
    block_recv,
    far_recv,
    ring_send,
    far_send,
    away_send,
    query_send,
    query_recv,
    rows_send,
    rows_recv,
    answer_send,
    answer_recv,
    gap_send,
    gap_recv,
):
    spans = 2 * levels
    half_way = levels // 2
    last = levels - 1
    me = lax.axis_index("mirror")
    core = lax.axis_index("tensor")
    z, y = me // 2, me % 2
    partner = z * 2 + 1 - y
    up = ((z + 1) % levels) * 2 + y
    down = ((z + levels - 1) % levels) * 2 + y
    mine_at = pl.multiple_of(y * HEAD, HEAD)
    away_at = pl.multiple_of((1 - y) * HEAD, HEAD)
    mine_q = y * GROUP * HEAD
    away_q = (1 - y) * GROUP * HEAD

    barrier = pltpu.get_barrier_semaphore()
    for other in (up, down, partner):
        pl.semaphore_signal(barrier, inc=1, device_id={"mirror": other})
    pl.semaphore_signal(barrier, inc=1, device_id={"tensor": 1 - core})

    def q_columns(at, g):
        return q_h.at[:, pl.ds(pl.multiple_of(at + g * HEAD, HEAD), HEAD)]

    def load(src, dst, i):
        return pltpu.make_async_copy(src, dst, load_sem.at[i])

    loads = [
        load(sel_h, sel_ref, 0),
        load(order_h, order_v, 1),
        load(counts_h, counts_v, 2),
        load(k_h, k_ref, 3),
        load(v_h, v_ref, 4),
    ]
    later = [
        load(order_h, order_s, 5),
        load(counts_h, counts_s, 6),
        load(rk_h.at[:, pl.ds(mine_at, HEAD)], fresh.at[0, 0, 0], 7),
        load(rv_h.at[:, pl.ds(mine_at, HEAD)], fresh.at[0, 1, 0], 8),
    ]
    for copy in loads:
        copy.start()

    def load_query(g):
        return pltpu.make_async_copy(
            q_columns(mine_q, g), queries.at[0, pl.ds(g * ROWS, ROWS), :], query_load.at[g]
        )

    def send(src, dst, send_sem, recv_sem, to):
        return pltpu.make_async_remote_copy(
            src_ref=src, dst_ref=dst, send_sem=send_sem, recv_sem=recv_sem, device_id=to
        )

    def rows_of(unit, slot):
        return fresh.at[unit, :, slot]

    def kept_of(unit, slot):
        return kept.at[unit, :, slot, pl.ds(0, KEPT), :]

    def way(direction):
        return {"mirror": up if direction == 0 else down}

    def ring(direction, unit, slot, kind, to_unit):
        piece = (rows_of, kept_of)[kind]
        return send(
            piece(unit, slot), piece(to_unit, direction), ring_send.at[direction, to_unit, kind],
            block_recv.at[to_unit, direction, kind], way(direction),
        )

    def far(kv, half, kind, unit):
        if kind == 0:
            src, dst = fresh.at[unit, kv, kv], fresh.at[last, kv, half]
        else:
            src = kept.at[unit, kv, kv, pl.ds(0, KEPT), :]
            dst = kept.at[last, kv, half, pl.ds(0, KEPT), :]
        return send(src, dst, far_send.at[kv, half, kind], far_recv.at[kv, half, kind], way(kv))

    def arrived(unit, slot, kind):
        piece = (rows_of, kept_of)[kind]
        send(
            piece(unit, slot), piece(unit, slot), ring_send.at[0, 0, 0],
            block_recv.at[unit, slot, kind], way(0),
        ).wait_recv()

    pl.semaphore_wait(barrier, 4)

    for kv, rows_h in enumerate((rk_h, rv_h)):
        for direction in range(2):
            send(
                rows_h.at[:, pl.ds(mine_at, HEAD)], fresh.at[1, kv, direction],
                ring_send.at[direction, 1, 0], block_recv.at[1, direction, 0], way(direction),
            ).start()
        send(
            rows_h.at[:, pl.ds(away_at, HEAD)], fresh.at[0, kv, 1], away_send.at[0],
            block_recv.at[0, 1, 0], {"mirror": partner},
        ).start()
    for copy in loads:
        copy.wait()
    for copy in later:
        copy.start()

    sel_all = sel_ref[...].astype(F32)
    chosen = jnp.where(order_v[...] == me, 1.0, 0.0)
    my_sel = dot(jnp.broadcast_to(chosen, (8, spans)).astype(BF16), sel_all.astype(BF16))[:1]
    my_live = jnp.sum(chosen * counts_v[...].astype(F32), axis=1, keepdims=True)

    keep_mine = kept_rows(my_sel, my_live)[:KEPT]
    for kv, cache in enumerate((k_ref, v_ref)):
        away[kv] = dot(keep_mine, cache[:, pl.ds(away_at, HEAD)]).astype(BF16)
    across = send(
        away, kept_of(0, 1), away_send.at[1], block_recv.at[0, 1, 1], {"mirror": partner}
    )
    across.start()
    for kv, cache in enumerate((k_ref, v_ref)):
        kept[0, kv, 0, 0:KEPT, :] = dot(keep_mine, cache[:, pl.ds(mine_at, HEAD)]).astype(BF16)
    for direction in range(2):
        ring(direction, 0, 0, 1, 1).start()

    def ask(g):
        return send(
            q_columns(away_q, g), queries.at[1, pl.ds(g * ROWS, ROWS), :],
            query_send.at[g], query_recv.at[g], {"mirror": partner},
        )

    for g in range(GROUP):
        load_query(g).start()
    for copy in later:
        copy.wait()
    arrived(0, 1, 0)
    for direction in range(2):
        ring(direction, 0, 1, 0, 2).start()
    acc[...] = jnp.zeros_like(acc)
    total[...] = jnp.zeros_like(total)
    top[...] = jnp.full_like(top, LOW)
    kept[:, 1, :, KEPT:, :] = jnp.zeros((levels, 2, TOKENS - KEPT, HEAD), BF16)

    counts_f = counts_v[...].astype(F32)
    c_at, s_at = iota((spans, spans), 0), iota((spans, spans), 1)
    pick = order_v[...].astype(F32) == c_at
    slot_of = jnp.sum(jnp.where(pick, s_at, 0.0), axis=1, keepdims=True)
    slot_live = jnp.sum(jnp.where(pick, counts_f, 0.0), axis=1, keepdims=True)
    row_live = jnp.sum(jnp.where(c_at == s_at, counts_f, 0.0), axis=1, keepdims=True)
    span_at = iota((spans, ROWS), 0)[:, :1]
    for o, slot in ((0, me), (1, partner)):
        at = slot.astype(F32)
        live = counts_s[0, slot].astype(F32)
        sel_row = sel_ref[pl.ds(slot, 1), :].astype(F32)
        limit[o] = turn(sel_row)
        places = iota((8, TOKENS), 1).astype(BF16)
        diagonal = dot_nt(places, kept_rows(sel_row, live))[:1]
        end = jnp.where(slot_of <= at, jnp.minimum(TOKENS - slot_live, float(KEPT)), 0.0)
        same = jnp.where(slot_of == at, 1.0, 0.0)
        token_kept[o] = jnp.where(iota((spans, TOKENS), 1) < end, same * diagonal, FAR)
        end = jnp.where(span_at <= at, row_live, 0.0)
        same = jnp.where(span_at == at, 1.0, 0.0)
        token_fresh[o] = jnp.where(iota((spans, ROWS), 1) < end, same * sel_row, FAR)

    across.wait_send()
    for g in range(GROUP):
        ask(g).start()
    arrived(0, 1, 1)
    for direction in range(2):
        ring(direction, 0, 1, 1, 2).start()
    for g in range(GROUP):
        load_query(g).wait()

    def attend(o, spans_at, keys, values, after=None):
        tokens = jnp.concatenate(
            [token_kept[o, pl.ds(c, 1), :] for c in spans_at]
            + [token_fresh[o, pl.ds(c, 1), :] for c in spans_at],
            axis=1,
        )
        wide = tokens.shape[1]
        split = keys[0].shape[0]
        bound = limit[o]
        seen = jnp.concatenate(
            [tokens[:, j:j + HEAD] <= bound for j in range(0, wide, HEAD)], axis=1
        )
        values = [jnp.concatenate([v, jnp.ones_like(v)], axis=1) for v in values]
        for t in range(GROUP * ROWS // TILE):
            rows = slice(t * TILE, (t + 1) * TILE)
            q = queries[o, rows, :]
            scores = jnp.concatenate([dot_nt(q, k) for k in keys], axis=1) * SCALE
            scores = scores.reshape(TILE // ROWS, ROWS, wide)
            scores = jnp.where(seen[None], scores, LOW).reshape(TILE, wide)
            old = top[o, rows, :]
            new = jnp.maximum(old, jnp.max(scores, axis=1, keepdims=True))
            decay = jnp.exp2(old - new)
            weights = jnp.exp2(scores - jnp.concatenate([new] * (wide // HEAD), axis=1))
            weights = weights.astype(BF16)
            found = dot(weights[:, :split], values[0]) + dot(weights[:, split:], values[1])
            sums = total[o, rows, :] * decay + found[:, HEAD:]
            mixed = acc[o, rows, :] * decay + found[:, :HEAD]
            if after is not None:
                after(t, mixed / sums)
            else:
                top[o, rows, :] = new
                total[o, rows, :] = sums
                acc[o, rows, :] = mixed

    def absorb(unit, o):
        distance = (unit + 1) // 2
        half = jnp.where(unit == 0, 0, (unit + 1) % 2)
        column = (y + half) % 2
        whole = (unit == 0) | (unit == last)
        first = ((z + levels - distance) % levels) * 2 + jnp.where(whole, y, column)
        second = ((z + distance) % levels) * 2 + jnp.where(whole, 1 - y, column)
        both = [
            (kept[unit, kv].reshape(2 * TOKENS, HEAD), fresh[unit, kv].reshape(2 * ROWS, HEAD))
            for kv in range(2)
        ]
        attend(o, (first, second), *both)

    def relay(unit):
        for kind in range(2):
            for direction in range(2):
                arrived(unit, direction, kind)

                @pl.when(unit < last - 2)
                def _():
                    ring(direction, unit, direction, kind, unit + 2).start()

                @pl.when(unit >= last - 2)
                def _():
                    far(direction, (unit + 1) % 2, kind, unit).start()

    def find(s, found):
        return tuple(
            jnp.where(order_s[0, s] == span, s, slot) for span, slot in zip((me, partner), found)
        )

    my_slot, partner_slot = lax.fori_loop(0, spans, find, (0, 0))

    def early(i, carry):
        for at, unit in ((0, 1), (1, 2), (3, 3)):
            @pl.when(i == at)
            def _():
                relay(unit)

        @pl.when(i == 2)
        def _():
            for g in range(GROUP):
                ask(g).wait_recv()

        o = jnp.where((i >= 2) & (i <= 4), 1, 0)
        absorb(jnp.where(i < 2, i, jnp.where(i < 5, i - 2, 2)), o)
        return carry

    lax.fori_loop(0, 6, early, 0)

    def step(unit, carry):
        relay(unit)
        for o in (1, 0):
            absorb(unit - 1, o)
        return carry

    lax.fori_loop(4, last - 1, step, 0)
    relay(last - 1)

    def late(unit, carry):
        absorb(unit, 1)
        return carry

    lax.fori_loop(last - 2, last, late, 0)

    def out_columns(g):
        return out_h.at[:, pl.ds(pl.multiple_of(mine_q + g * HEAD, HEAD), HEAD)]

    def reply(g):
        return send(
            answer.at[g],
            out_columns(g),
            answer_send.at[g], answer_recv.at[g], {"mirror": partner},
        )

    def far_half(half, after=None):
        attend(
            1,
            (((z + half_way) % levels) * 2 + (y + half) % 2,),
            *[(kept[last, kv, half], fresh[last, kv, half]) for kv in range(2)],
            after=after,
        )

    def far_arrived(half, kind):
        for kv in range(2):
            far(kv, half, kind, last).wait_recv()

    far_arrived(0, 0)
    far_arrived(0, 1)
    far_half(0)
    far_arrived(1, 0)

    def where_is(slot):
        half = (slot + y) % 2
        ahead = (slot // 2 + levels - z) % levels
        distance = jnp.minimum(ahead, levels - ahead)
        whole = (ahead == 0) | (ahead == half_way)
        unit = jnp.where(ahead == 0, 0, jnp.where(ahead == half_way, last, 2 * distance - 1 + half))
        side = jnp.where(whole, half, jnp.where(ahead < half_way, 1, 0))
        return unit, side

    unit, side = where_is(partner_slot)
    for kv in range(2):
        rows_out[kv] = fresh[unit, kv, side]
    hand = send(rows_out, rows_in, rows_send, rows_recv, {"mirror": partner})
    hand.start()

    far_arrived(1, 1)
    partner_live = counts_s[0, partner].astype(F32)
    own_live = counts_s[0, me].astype(F32)

    def live_only(result, live):
        return jnp.where(iota((ROWS, HEAD), 0) < live, result, 0.0).astype(BF16)

    def give_back(t, result):
        for i in range(TILE // ROWS):
            g = t * (TILE // ROWS) + i
            answer[g] = live_only(result[i * ROWS:(i + 1) * ROWS], partner_live)
            reply(g).start()

    far_half(1, give_back)

    unit, side = where_is(my_slot)
    match = (iota((TOKENS, ROWS), 0) == my_sel) & (iota((TOKENS, ROWS), 1) < my_live)
    markers = jnp.where(match, 1.0, 0.0)
    hit = jnp.max(markers, axis=1, keepdims=True)
    markers = markers.astype(BF16)
    side_sel = turn(my_sel)
    side_sel = jnp.concatenate([side_sel, side_sel], axis=1)
    match = (iota((ROWS, TOKENS), 1) == side_sel) & (iota((ROWS, TOKENS), 0) < my_live)
    markers_t = jnp.where(match, 1.0, 0.0).astype(BF16)

    def blend(new_rows, cache, result, at):
        moved = dot(markers, new_rows)
        old = cache[:, pl.ds(at, HEAD)]
        result[:, pl.ds(at, HEAD)] = jnp.where(hit > 0.5, moved, old.astype(F32)).astype(BF16)

    def gaps(new_rows, at):
        gap = new_rows.astype(F32) - dot(markers_t, k_ref[:, pl.ds(at, HEAD)])
        return jnp.sum(gap * gap, axis=1, keepdims=True)

    fresh_k = fresh[unit, 0, side]
    fresh_v = fresh[unit, 1, side]
    hand.wait_recv()
    squares = gaps(fresh_k, mine_at) + gaps(rows_in[0], away_at)
    gap_mine[...] = jnp.broadcast_to(squares, (ROWS, ROWS)).T[:8]
    swap = send(gap_mine, gap_other, gap_send, gap_recv, {"tensor": 1 - core})
    swap.start()
    blend(fresh_k, k_ref, mk_ref, mine_at)
    blend(fresh_v, v_ref, mv_ref, mine_at)
    blend(rows_in[0], k_ref, mk_ref, away_at)
    blend(rows_in[1], v_ref, mv_ref, away_at)

    stores = [
        pltpu.make_async_copy(mk_ref, mk_h, store_sem.at[0]),
        pltpu.make_async_copy(mv_ref, mv_h, store_sem.at[1]),
    ]
    for store in stores:
        store.start()

    def own_rest(unit, carry):
        absorb(unit, 0)
        return carry

    lax.fori_loop(last - 2, levels, own_rest, 0)
    def keep(g):
        return pltpu.make_async_copy(own_out.at[g], out_columns(g), own_sem.at[g])

    for g in range(GROUP):
        rows = slice(g * ROWS, (g + 1) * ROWS)
        own_out[g] = live_only(acc[0, rows, :] / total[0, rows, :], own_live)
        keep(g).start()
    swap.wait_recv()
    mean = (gap_mine[:1] + gap_other[:1]) / (4.0 * HEAD)
    dev_ref[...] = jnp.where(iota((1, ROWS), 1) < my_live, mean, 0.0)
    store_dev = pltpu.make_async_copy(dev_ref, dev_h, store_sem.at[2])
    store_dev.start()

    swap.wait_send()
    hand.wait_send()
    send(
        rows_of(0, 1), rows_of(0, 1), away_send.at[0], block_recv.at[0, 1, 0], way(0)
    ).wait_send()
    for kv in range(2):
        for half in range(2):
            for kind in range(2):
                far(kv, half, kind, last).wait_send()

    def drain(unit, carry):
        for direction in range(2):
            for kind in range(2):
                ring(direction, unit, direction, kind, unit).wait_send()
        return carry

    lax.fori_loop(1, last, drain, 0)
    for g in range(GROUP):
        ask(g).wait_send()
    for store in stores + [store_dev] + [keep(g) for g in range(GROUP)]:
        store.wait()
    for g in range(GROUP):
        reply(g).wait_recv()
        reply(g).wait_send()


def deliver(*refs):
    count = (len(refs) - 2) // 3
    held, sems_in, sems_out = refs[2 * count:3 * count], refs[-2], refs[-1]
    takes = [
        pltpu.make_async_copy(refs[i], held[i], sems_in.at[i]) for i in range(count)
    ]
    gives = [
        pltpu.make_async_copy(held[i], refs[count + i], sems_out.at[i]) for i in range(count)
    ]
    for take in takes:
        take.start()
    for take, give in zip(takes, gives):
        take.wait()
        give.start()
    for give in gives:
        give.wait()


def body(k_cache, value_cache, queries, new_keys, new_values, sel_index, counts, span_order):
    spans = sel_index.shape[0]
    levels = spans // 2
    columns = queries.shape[2]
    wide = k_cache.shape[2]
    hbm = pl.BlockSpec(memory_space=pltpu.HBM)
    dma = pltpu.SemaphoreType.DMA
    stats = pltpu.VMEM((2, GROUP * ROWS, HEAD), F32)
    shapes = (
        jax.ShapeDtypeStruct((ROWS, columns), BF16),
        jax.ShapeDtypeStruct((TOKENS, wide), BF16),
        jax.ShapeDtypeStruct((TOKENS, wide), BF16),
        jax.ShapeDtypeStruct((1, ROWS), F32),
    )
    results = pl.pallas_call(
        functools.partial(kernel, levels),
        out_shape=shapes,
        in_specs=[hbm] * 8,
        out_specs=(hbm,) * 4,
        scratch_shapes=[
            pltpu.VMEM((TOKENS, wide), BF16),
            pltpu.VMEM((TOKENS, wide), BF16),
            pltpu.VMEM((1, ROWS), F32),
            pltpu.SMEM((1, spans), jnp.int32),
            pltpu.SMEM((1, spans), jnp.int32),
            pltpu.VMEM((1, spans), jnp.int32),
            pltpu.VMEM((1, spans), jnp.int32),
            pltpu.VMEM((spans, ROWS), jnp.int32),
            pltpu.VMEM((TOKENS, wide), BF16),
            pltpu.VMEM((TOKENS, wide), BF16),
            pltpu.VMEM((levels, 2, 2, TOKENS, HEAD), BF16),
            pltpu.VMEM((levels, 2, 2, ROWS, HEAD), BF16),
            pltpu.VMEM((2, GROUP * ROWS, HEAD), BF16),
            stats,
            stats,
            stats,
            pltpu.VMEM((2, spans, TOKENS), F32),
            pltpu.VMEM((2, spans, ROWS), F32),
            pltpu.VMEM((2, ROWS, ROWS), F32),
            pltpu.VMEM((2, KEPT, HEAD), BF16),
            pltpu.VMEM((2, ROWS, HEAD), BF16),
            pltpu.VMEM((2, ROWS, HEAD), BF16),
            pltpu.VMEM((GROUP, ROWS, HEAD), BF16),
            pltpu.VMEM((GROUP, ROWS, HEAD), BF16),
            pltpu.VMEM((8, ROWS), F32),
            pltpu.VMEM((8, ROWS), F32),
            dma((9,)),
            dma((3,)),
            dma((GROUP,)),
            dma((GROUP,)),
            dma((levels, 2, 2)),
            dma((2, 2, 2)),
            dma((2, levels, 2)),
            dma((2, 2, 2)),
            dma((2,)),
            dma((GROUP,)),
            dma((GROUP,)),
            dma,
            dma,
            dma((GROUP,)),
            dma((GROUP,)),
            dma,
            dma,
        ],
        compiler_params=pltpu.CompilerParams(
            collective_id=0, has_side_effects=True, vmem_limit_bytes=VMEM_BYTES
        ),
    )(
        span_order[None],
        counts[None],
        sel_index,
        k_cache[0],
        value_cache[0],
        queries[0],
        new_keys[0],
        new_values[0],
    )
    out, mk, mv, dev = pl.pallas_call(
        deliver,
        out_shape=shapes,
        in_specs=[hbm] * 4,
        out_specs=(hbm,) * 4,
        scratch_shapes=[pltpu.VMEM(a.shape, a.dtype) for a in shapes] + [dma((4,)), dma((4,))],
        compiler_params=pltpu.CompilerParams(vmem_limit_bytes=VMEM_BYTES),
    )(*results)
    return out[None], mk[None], mv[None], dev


def solution(mesh):
    whole = P(("request", "mirror"), None, "tensor")
    in_specs = (whole,) * 5 + (P("request", None), P("request"), P("request"))
    out_specs = (whole, whole, whole, P(("request", "mirror"), None))
    return jax.shard_map(body, mesh=mesh, in_specs=in_specs, out_specs=out_specs, check_vma=False)
```

```python
import functools
import math

import jax
import jax.numpy as jnp
from jax import lax
from jax.experimental import pallas as pl
from jax.experimental.pallas import tpu as pltpu
from jax.sharding import PartitionSpec as P

HEAD = 128
TOKENS = 256
ROWS = 128
LEAST = 48
KEPT = TOKENS - LEAST
GROUP = 8
VMEM_BYTES = 64 * 2**20 - 2**17
TILE = 256
LOW = -1e30
FAR = 1e9
SCALE = math.log2(math.e) / math.sqrt(HEAD)
F32 = jnp.float32
BF16 = jnp.bfloat16


def dot(a, b):
    return jnp.dot(a, b, preferred_element_type=F32)


def dot_nt(a, b):
    return lax.dot_general(a, b, (((1,), (1,)), ((), ())), preferred_element_type=F32)


def iota(shape, dim):
    return lax.broadcasted_iota(jnp.int32, shape, dim).astype(F32)


def turn(row):
    return jnp.broadcast_to(row, (ROWS, ROWS)).T


def kept_rows(sel_row, live):
    places = iota((ROWS, TOKENS), 1)
    side = turn(sel_row)
    side = jnp.concatenate([side, side], axis=1)
    slots = iota((ROWS, TOKENS), 0)
    hits = jnp.where((places == side) & (slots < live), 1.0, 0.0)
    keep = 1.0 - jnp.max(hits, axis=0, keepdims=True)
    before = jnp.where(iota((TOKENS, TOKENS), 0) < iota((TOKENS, TOKENS), 1), 1.0, 0.0)
    rank = dot(jnp.broadcast_to(keep, (8, TOKENS)).astype(BF16), before.astype(BF16))[:1]
    rank = jnp.where(keep > 0.5, rank, -1.0)
    return jnp.where(iota((TOKENS, TOKENS), 0) == rank, 1.0, 0.0).astype(BF16)


def kernel(
    levels,
    order_h,
    counts_h,
    sel_h,
    k_h,
    v_h,
    q_h,
    rk_h,
    rv_h,
    out_h,
    mk_h,
    mv_h,
    dev_h,
    mk_ref,
    mv_ref,
    dev_ref,
    order_s,
    counts_s,
    order_v,
    counts_v,
    sel_ref,
    k_ref,
    v_ref,
    kept,
    fresh,
    queries,
    acc,
    total,
    top,
    token_kept,
    token_fresh,
    limit,
    away,
    rows_out,
    rows_in,
    answer,
    own_out,
    gap_mine,
    gap_other,
    load_sem,
    store_sem,
    own_sem,
    query_load,
    block_recv,
    far_recv,
    ring_send,
    far_send,
    away_send,
    query_send,
    query_recv,
    rows_send,
    rows_recv,
    answer_send,
    answer_recv,
    gap_send,
    gap_recv,
):
    spans = 2 * levels
    half_way = levels // 2
    last = levels - 1
    me = lax.axis_index("mirror")
    core = lax.axis_index("tensor")
    z, y = me // 2, me % 2
    partner = z * 2 + 1 - y
    up = ((z + 1) % levels) * 2 + y
    down = ((z + levels - 1) % levels) * 2 + y
    mine_at = pl.multiple_of(y * HEAD, HEAD)
    away_at = pl.multiple_of((1 - y) * HEAD, HEAD)
    mine_q = y * GROUP * HEAD
    away_q = (1 - y) * GROUP * HEAD

    barrier = pltpu.get_barrier_semaphore()
    for other in (up, down, partner):
        pl.semaphore_signal(barrier, inc=1, device_id={"mirror": other})
    pl.semaphore_signal(barrier, inc=1, device_id={"tensor": 1 - core})

    def q_columns(at, g):
        return q_h.at[:, pl.ds(pl.multiple_of(at + g * HEAD, HEAD), HEAD)]

    def load(src, dst, i):
        return pltpu.make_async_copy(src, dst, load_sem.at[i])

    loads = [
        load(sel_h, sel_ref, 0),
        load(order_h, order_v, 1),
        load(counts_h, counts_v, 2),
        load(k_h, k_ref, 3),
        load(v_h, v_ref, 4),
    ]
    later = [
        load(order_h, order_s, 5),
        load(counts_h, counts_s, 6),
        load(rk_h.at[:, pl.ds(mine_at, HEAD)], fresh.at[0, 0, 0], 7),
        load(rv_h.at[:, pl.ds(mine_at, HEAD)], fresh.at[0, 1, 0], 8),
    ]
    for copy in loads:
        copy.start()

    def load_query(g):
        return pltpu.make_async_copy(
            q_columns(mine_q, g), queries.at[0, pl.ds(g * ROWS, ROWS), :], query_load.at[g]
        )

    def send(src, dst, send_sem, recv_sem, to):
        return pltpu.make_async_remote_copy(
            src_ref=src, dst_ref=dst, send_sem=send_sem, recv_sem=recv_sem, device_id=to
        )

    def rows_of(unit, slot):
        return fresh.at[unit, :, slot]

    def kept_of(unit, slot):
        return kept.at[unit, :, slot, pl.ds(0, KEPT), :]

    def way(direction):
        return {"mirror": up if direction == 0 else down}

    def ring(direction, unit, slot, kind, to_unit):
        piece = (rows_of, kept_of)[kind]
        return send(
            piece(unit, slot), piece(to_unit, direction), ring_send.at[direction, to_unit, kind],
            block_recv.at[to_unit, direction, kind], way(direction),
        )

    def far(kv, half, kind, unit):
        if kind == 0:
            src, dst = fresh.at[unit, kv, kv], fresh.at[last, kv, half]
        else:
            src = kept.at[unit, kv, kv, pl.ds(0, KEPT), :]
            dst = kept.at[last, kv, half, pl.ds(0, KEPT), :]
        return send(src, dst, far_send.at[kv, half, kind], far_recv.at[kv, half, kind], way(kv))

    def arrived(unit, slot, kind):
        piece = (rows_of, kept_of)[kind]
        send(
            piece(unit, slot), piece(unit, slot), ring_send.at[0, 0, 0],
            block_recv.at[unit, slot, kind], way(0),
        ).wait_recv()

    pl.semaphore_wait(barrier, 4)

    for kv, rows_h in enumerate((rk_h, rv_h)):
        for direction in range(2):
            send(
                rows_h.at[:, pl.ds(mine_at, HEAD)], fresh.at[1, kv, direction],
                ring_send.at[direction, 1, 0], block_recv.at[1, direction, 0], way(direction),
            ).start()
        send(
            rows_h.at[:, pl.ds(away_at, HEAD)], fresh.at[0, kv, 1], away_send.at[0],
            block_recv.at[0, 1, 0], {"mirror": partner},
        ).start()
    for copy in loads:
        copy.wait()
    for copy in later:
        copy.start()

    sel_all = sel_ref[...].astype(F32)
    chosen = jnp.where(order_v[...] == me, 1.0, 0.0)
    my_sel = dot(jnp.broadcast_to(chosen, (8, spans)).astype(BF16), sel_all.astype(BF16))[:1]
    my_live = jnp.sum(chosen * counts_v[...].astype(F32), axis=1, keepdims=True)

    keep_mine = kept_rows(my_sel, my_live)[:KEPT]
    for kv, cache in enumerate((k_ref, v_ref)):
        kept[0, kv, 0, 0:KEPT, :] = dot(keep_mine, cache[:, pl.ds(mine_at, HEAD)]).astype(BF16)
    for direction in range(2):
        ring(direction, 0, 0, 1, 1).start()
    for kv, cache in enumerate((k_ref, v_ref)):
        away[kv] = dot(keep_mine, cache[:, pl.ds(away_at, HEAD)]).astype(BF16)
    across = send(
        away, kept_of(0, 1), away_send.at[1], block_recv.at[0, 1, 1], {"mirror": partner}
    )
    across.start()

    def ask(g):
        return send(
            q_columns(away_q, g), queries.at[1, pl.ds(g * ROWS, ROWS), :],
            query_send.at[g], query_recv.at[g], {"mirror": partner},
        )

    for g in range(GROUP):
        load_query(g).start()
    for copy in later:
        copy.wait()
    arrived(0, 1, 0)
    for direction in range(2):
        ring(direction, 0, 1, 0, 2).start()
    acc[...] = jnp.zeros_like(acc)
    total[...] = jnp.zeros_like(total)
    top[...] = jnp.full_like(top, LOW)
    kept[:, 1, :, KEPT:, :] = jnp.zeros((levels, 2, TOKENS - KEPT, HEAD), BF16)

    def relay(unit, kinds=(0, 1)):
        for kind in kinds:
            for direction in range(2):
                arrived(unit, direction, kind)

                @pl.when(unit < last - 2)
                def _():
                    ring(direction, unit, direction, kind, unit + 2).start()

                @pl.when(unit >= last - 2)
                def _():
                    far(direction, (unit + 1) % 2, kind, unit).start()

    counts_f = counts_v[...].astype(F32)
    c_at, s_at = iota((spans, spans), 0), iota((spans, spans), 1)
    pick = order_v[...].astype(F32) == c_at
    slot_of = jnp.sum(jnp.where(pick, s_at, 0.0), axis=1, keepdims=True)
    slot_live = jnp.sum(jnp.where(pick, counts_f, 0.0), axis=1, keepdims=True)
    row_live = jnp.sum(jnp.where(c_at == s_at, counts_f, 0.0), axis=1, keepdims=True)
    span_at = iota((spans, ROWS), 0)[:, :1]
    for o, slot in ((0, me), (1, partner)):
        at = slot.astype(F32)
        live = counts_s[0, slot].astype(F32)
        sel_row = sel_ref[pl.ds(slot, 1), :].astype(F32)
        limit[o] = turn(sel_row)
        places = iota((8, TOKENS), 1).astype(BF16)
        diagonal = dot_nt(places, kept_rows(sel_row, live))[:1]
        end = jnp.where(slot_of <= at, jnp.minimum(TOKENS - slot_live, float(KEPT)), 0.0)
        same = jnp.where(slot_of == at, 1.0, 0.0)
        token_kept[o] = jnp.where(iota((spans, TOKENS), 1) < end, same * diagonal, FAR)
        end = jnp.where(span_at <= at, row_live, 0.0)
        same = jnp.where(span_at == at, 1.0, 0.0)
        token_fresh[o] = jnp.where(iota((spans, ROWS), 1) < end, same * sel_row, FAR)

    relay(1, (0,))
    across.wait_send()
    for g in range(GROUP):
        ask(g).start()
    arrived(0, 1, 1)
    for direction in range(2):
        ring(direction, 0, 1, 1, 2).start()
    for g in range(GROUP):
        load_query(g).wait()

    def attend(o, spans_at, keys, values, after=None):
        tokens = jnp.concatenate(
            [token_kept[o, pl.ds(c, 1), :] for c in spans_at]
            + [token_fresh[o, pl.ds(c, 1), :] for c in spans_at],
            axis=1,
        )
        wide = tokens.shape[1]
        split = keys[0].shape[0]
        bound = limit[o]
        seen = jnp.concatenate(
            [tokens[:, j:j + HEAD] <= bound for j in range(0, wide, HEAD)], axis=1
        )
        values = [jnp.concatenate([v, jnp.ones_like(v)], axis=1) for v in values]
        for t in range(GROUP * ROWS // TILE):
            rows = slice(t * TILE, (t + 1) * TILE)
            q = queries[o, rows, :]
            scores = jnp.concatenate([dot_nt(q, k) for k in keys], axis=1) * SCALE
            scores = scores.reshape(TILE // ROWS, ROWS, wide)
            scores = jnp.where(seen[None], scores, LOW).reshape(TILE, wide)
            old = top[o, rows, :]
            new = jnp.maximum(old, jnp.max(scores, axis=1, keepdims=True))
            decay = jnp.exp2(old - new)
            weights = jnp.exp2(scores - jnp.concatenate([new] * (wide // HEAD), axis=1))
            weights = weights.astype(BF16)
            found = dot(weights[:, :split], values[0]) + dot(weights[:, split:], values[1])
            sums = total[o, rows, :] * decay + found[:, HEAD:]
            mixed = acc[o, rows, :] * decay + found[:, :HEAD]
            if after is not None:
                after(t, mixed / sums)
            else:
                top[o, rows, :] = new
                total[o, rows, :] = sums
                acc[o, rows, :] = mixed

    def absorb(unit, o):
        distance = (unit + 1) // 2
        half = jnp.where(unit == 0, 0, (unit + 1) % 2)
        column = (y + half) % 2
        whole = (unit == 0) | (unit == last)
        first = ((z + levels - distance) % levels) * 2 + jnp.where(whole, y, column)
        second = ((z + distance) % levels) * 2 + jnp.where(whole, 1 - y, column)
        both = [
            (kept[unit, kv].reshape(2 * TOKENS, HEAD), fresh[unit, kv].reshape(2 * ROWS, HEAD))
            for kv in range(2)
        ]
        attend(o, (first, second), *both)

    def find(s, found):
        return tuple(
            jnp.where(order_s[0, s] == span, s, slot) for span, slot in zip((me, partner), found)
        )

    my_slot, partner_slot = lax.fori_loop(0, spans, find, (0, 0))

    def own_first(unit, carry):
        @pl.when(unit == 1)
        def _():
            relay(1, (1,))

        @pl.when(unit == 2)
        def _():
            relay(2)

        absorb(unit, 0)
        return carry

    lax.fori_loop(0, 3, own_first, 0)
    for g in range(GROUP):
        ask(g).wait_recv()
    absorb(0, 1)

    def behind(unit, carry):
        relay(unit)
        absorb(unit, 0)
        absorb(unit - 2, 1)
        return carry

    def gaining(unit, carry):
        relay(unit)
        absorb(unit, 0)
        absorb(2 * unit - 7, 1)
        absorb(2 * unit - 6, 1)
        return carry

    def step(unit, carry):
        relay(unit)
        for o in (1, 0):
            absorb(unit, o)
        return carry

    gained = min(7, last - 1)
    lax.fori_loop(3, 5, behind, 0)
    lax.fori_loop(5, gained, gaining, 0)
    lax.fori_loop(gained, last - 1, step, 0)
    relay(last - 1)
    seen_by_partner = last - 1 if gained == 7 else 2 * gained - 7
    for unit in range(seen_by_partner, last):
        absorb(unit, 1)

    def out_columns(g):
        return out_h.at[:, pl.ds(pl.multiple_of(mine_q + g * HEAD, HEAD), HEAD)]

    def reply(g):
        return send(
            answer.at[g],
            out_columns(g),
            answer_send.at[g], answer_recv.at[g], {"mirror": partner},
        )

    def far_half(half, o, after=None):
        attend(
            o,
            (((z + half_way) % levels) * 2 + (y + half) % 2,),
            *[(kept[last, kv, half], fresh[last, kv, half]) for kv in range(2)],
            after=after,
        )

    def far_arrived(half, kind):
        for kv in range(2):
            far(kv, half, kind, last).wait_recv()

    far_arrived(0, 0)
    far_arrived(0, 1)
    far_half(0, 1)
    far_arrived(1, 0)

    def where_is(slot):
        half = (slot + y) % 2
        ahead = (slot // 2 + levels - z) % levels
        distance = jnp.minimum(ahead, levels - ahead)
        whole = (ahead == 0) | (ahead == half_way)
        unit = jnp.where(ahead == 0, 0, jnp.where(ahead == half_way, last, 2 * distance - 1 + half))
        side = jnp.where(whole, half, jnp.where(ahead < half_way, 1, 0))
        return unit, side

    unit, side = where_is(partner_slot)
    for kv in range(2):
        rows_out[kv] = fresh[unit, kv, side]
    hand = send(rows_out, rows_in, rows_send, rows_recv, {"mirror": partner})
    hand.start()
    far_half(0, 0)

    far_arrived(1, 1)
    partner_live = counts_s[0, partner].astype(F32)
    own_live = counts_s[0, me].astype(F32)

    def live_only(result, live):
        return jnp.where(iota((ROWS, HEAD), 0) < live, result, 0.0).astype(BF16)

    def give_back(t, result):
        for i in range(TILE // ROWS):
            g = t * (TILE // ROWS) + i
            answer[g] = live_only(result[i * ROWS:(i + 1) * ROWS], partner_live)
            reply(g).start()

    far_half(1, 1, give_back)

    def keep(g):
        return pltpu.make_async_copy(own_out.at[g], out_columns(g), own_sem.at[g])

    def keep_tile(t, result):
        for i in range(TILE // ROWS):
            g = t * (TILE // ROWS) + i
            own_out[g] = live_only(result[i * ROWS:(i + 1) * ROWS], own_live)
            keep(g).start()

    absorb(last - 1, 0)
    far_half(1, 0, keep_tile)

    unit, side = where_is(my_slot)
    match = (iota((TOKENS, ROWS), 0) == my_sel) & (iota((TOKENS, ROWS), 1) < my_live)
    markers = jnp.where(match, 1.0, 0.0)
    hit = jnp.max(markers, axis=1, keepdims=True)
    markers = markers.astype(BF16)
    side_sel = turn(my_sel)
    side_sel = jnp.concatenate([side_sel, side_sel], axis=1)
    match = (iota((ROWS, TOKENS), 1) == side_sel) & (iota((ROWS, TOKENS), 0) < my_live)
    markers_t = jnp.where(match, 1.0, 0.0).astype(BF16)

    def blend(new_rows, cache, result, at):
        moved = dot(markers, new_rows)
        old = cache[:, pl.ds(at, HEAD)]
        result[:, pl.ds(at, HEAD)] = jnp.where(hit > 0.5, moved, old.astype(F32)).astype(BF16)

    def gaps(new_rows, at):
        gap = new_rows.astype(F32) - dot(markers_t, k_ref[:, pl.ds(at, HEAD)])
        return jnp.sum(gap * gap, axis=1, keepdims=True)

    fresh_k = fresh[unit, 0, side]
    fresh_v = fresh[unit, 1, side]
    hand.wait_recv()
    squares = gaps(fresh_k, mine_at) + gaps(rows_in[0], away_at)
    gap_mine[...] = jnp.broadcast_to(squares, (ROWS, ROWS)).T[:8]
    swap = send(gap_mine, gap_other, gap_send, gap_recv, {"tensor": 1 - core})
    swap.start()
    blend(fresh_k, k_ref, mk_ref, mine_at)
    blend(fresh_v, v_ref, mv_ref, mine_at)
    blend(rows_in[0], k_ref, mk_ref, away_at)
    blend(rows_in[1], v_ref, mv_ref, away_at)

    stores = [
        pltpu.make_async_copy(mk_ref, mk_h, store_sem.at[0]),
        pltpu.make_async_copy(mv_ref, mv_h, store_sem.at[1]),
    ]
    for store in stores:
        store.start()

    swap.wait_recv()
    mean = (gap_mine[:1] + gap_other[:1]) / (4.0 * HEAD)
    dev_ref[...] = jnp.where(iota((1, ROWS), 1) < my_live, mean, 0.0)
    store_dev = pltpu.make_async_copy(dev_ref, dev_h, store_sem.at[2])
    store_dev.start()

    swap.wait_send()
    hand.wait_send()
    send(
        rows_of(0, 1), rows_of(0, 1), away_send.at[0], block_recv.at[0, 1, 0], way(0)
    ).wait_send()
    for kv in range(2):
        for half in range(2):
            for kind in range(2):
                far(kv, half, kind, last).wait_send()

    def drain(unit, carry):
        for direction in range(2):
            for kind in range(2):
                ring(direction, unit, direction, kind, unit).wait_send()
        return carry

    lax.fori_loop(1, last, drain, 0)
    for g in range(GROUP):
        ask(g).wait_send()
    for store in stores + [store_dev] + [keep(g) for g in range(GROUP)]:
        store.wait()
    for g in range(GROUP):
        reply(g).wait_recv()
        reply(g).wait_send()


def deliver(*refs):
    count = (len(refs) - 2) // 3
    held, sems_in, sems_out = refs[2 * count:3 * count], refs[-2], refs[-1]
    takes = [
        pltpu.make_async_copy(refs[i], held[i], sems_in.at[i]) for i in range(count)
    ]
    gives = [
        pltpu.make_async_copy(held[i], refs[count + i], sems_out.at[i]) for i in range(count)
    ]
    for take in takes:
        take.start()
    for take, give in zip(takes, gives):
        take.wait()
        give.start()
    for give in gives:
        give.wait()


def body(k_cache, value_cache, queries, new_keys, new_values, sel_index, counts, span_order):
    spans = sel_index.shape[0]
    levels = spans // 2
    columns = queries.shape[2]
    wide = k_cache.shape[2]
    hbm = pl.BlockSpec(memory_space=pltpu.HBM)
    dma = pltpu.SemaphoreType.DMA
    stats = pltpu.VMEM((2, GROUP * ROWS, HEAD), F32)
    shapes = (
        jax.ShapeDtypeStruct((ROWS, columns), BF16),
        jax.ShapeDtypeStruct((TOKENS, wide), BF16),
        jax.ShapeDtypeStruct((TOKENS, wide), BF16),
        jax.ShapeDtypeStruct((1, ROWS), F32),
    )
    results = pl.pallas_call(
        functools.partial(kernel, levels),
        out_shape=shapes,
        in_specs=[hbm] * 8,
        out_specs=(hbm,) * 4,
        scratch_shapes=[
            pltpu.VMEM((TOKENS, wide), BF16),
            pltpu.VMEM((TOKENS, wide), BF16),
            pltpu.VMEM((1, ROWS), F32),
            pltpu.SMEM((1, spans), jnp.int32),
            pltpu.SMEM((1, spans), jnp.int32),
            pltpu.VMEM((1, spans), jnp.int32),
            pltpu.VMEM((1, spans), jnp.int32),
            pltpu.VMEM((spans, ROWS), jnp.int32),
            pltpu.VMEM((TOKENS, wide), BF16),
            pltpu.VMEM((TOKENS, wide), BF16),
            pltpu.VMEM((levels, 2, 2, TOKENS, HEAD), BF16),
            pltpu.VMEM((levels, 2, 2, ROWS, HEAD), BF16),
            pltpu.VMEM((2, GROUP * ROWS, HEAD), BF16),
            stats,
            stats,
            stats,
            pltpu.VMEM((2, spans, TOKENS), F32),
            pltpu.VMEM((2, spans, ROWS), F32),
            pltpu.VMEM((2, ROWS, ROWS), F32),
            pltpu.VMEM((2, KEPT, HEAD), BF16),
            pltpu.VMEM((2, ROWS, HEAD), BF16),
            pltpu.VMEM((2, ROWS, HEAD), BF16),
            pltpu.VMEM((GROUP, ROWS, HEAD), BF16),
            pltpu.VMEM((GROUP, ROWS, HEAD), BF16),
            pltpu.VMEM((8, ROWS), F32),
            pltpu.VMEM((8, ROWS), F32),
            dma((9,)),
            dma((3,)),
            dma((GROUP,)),
            dma((GROUP,)),
            dma((levels, 2, 2)),
            dma((2, 2, 2)),
            dma((2, levels, 2)),
            dma((2, 2, 2)),
            dma((2,)),
            dma((GROUP,)),
            dma((GROUP,)),
            dma,
            dma,
            dma((GROUP,)),
            dma((GROUP,)),
            dma,
            dma,
        ],
        compiler_params=pltpu.CompilerParams(
            collective_id=0, has_side_effects=True, vmem_limit_bytes=VMEM_BYTES
        ),
    )(
        span_order[None],
        counts[None],
        sel_index,
        k_cache[0],
        value_cache[0],
        queries[0],
        new_keys[0],
        new_values[0],
    )
    out, mk, mv, dev = pl.pallas_call(
        deliver,
        out_shape=shapes,
        in_specs=[hbm] * 4,
        out_specs=(hbm,) * 4,
        scratch_shapes=[pltpu.VMEM(a.shape, a.dtype) for a in shapes] + [dma((4,)), dma((4,))],
        compiler_params=pltpu.CompilerParams(vmem_limit_bytes=VMEM_BYTES),
    )(*results)
    return out[None], mk[None], mv[None], dev


def solution(mesh):
    whole = P(("request", "mirror"), None, "tensor")
    in_specs = (whole,) * 5 + (P("request", None), P("request"), P("request"))
    out_specs = (whole, whole, whole, P(("request", "mirror"), None))
    return jax.shard_map(body, mesh=mesh, in_specs=in_specs, out_specs=out_specs, check_vma=False)
```
